512 devices in a mesh: out: 16 (over y, core), in: 32 (over z, x).
Axes of the slice: x: 4, y: 8, z: 8, core: 2. Of those that a mesh axis runs over, the one named last changes fastest.
Arguments:
- weight: float32 [16384, 16384], P('out', 'in'), may hold values from -6 to 6
- keep_tiles: int32 [128, 128], P('out', 'in'), may hold values from 0 to 1, as said below
- factor_rows: float32 [4, 256, 16384], P(None, 'out', 'in'), may hold values from -0.375 to 0.375
- diag_inverse: float32 [16384], P('in'), may hold values from 0.5 to 2
- block_order: int32 [4], replicated, may hold values from 0 to 63, as said below
Outputs:
- pruned_weight: float32 [16384, 16384], P('out', 'in')
The draws below stay inside these ranges and needn't reach their ends.
Inputs may be any that keep to these rules, and one draw needn't show every extreme that they name: `block_order`: distinct block numbers; the first and the last block are always among them. `keep_tiles`: for each index of out and each block of 256 inputs, the group of 16 tiles holds at most 10 zeros; in every block some group holds exactly 10.
All inputs are finite; a program needn't handle non-finite values.
Results may differ from the reference program's by a relative error of at most 0.0001.
Values sent between devices are 32-bit elements; how exact they have to be, the bound alone decides.
A program may use at most 64 MiB of HBM per device.

```python
import math
import jax
import jax.numpy as jnp
from jax import lax

C = 16384
TILE = 128
BLK = 256
R_DEV = 1024
NBLK = 4
MAXP = 10
R = 16384


def draw_keep_tiles(key, part):
    key = jax.random.fold_in(key, 11)
    key_count, key_force, key_score = jax.random.split(key, 3)
    row_tiles = R_DEV // TILE
    group = 2 * row_tiles
    groups = R // R_DEV
    blocks = C // BLK
    counts = jax.random.randint(key_count, (groups, blocks), group // 8, MAXP + 1)
    forced = jax.random.randint(key_force, (blocks,), 0, groups)
    counts = jnp.where(jnp.arange(groups)[:, None] == forced[None, :], MAXP, counts)
    scores = jax.random.randint(key_score, (groups, blocks, group), 0, 1 << 20) * group + jnp.arange(group)[None, None, :]
    ranks = jnp.argsort(jnp.argsort(scores, axis=2, stable=True), axis=2, stable=True)
    keep = jnp.where(ranks < counts[:, :, None], 0, 1).astype(jnp.int32)
    keep = keep.reshape(groups, blocks, row_tiles, 2).transpose(0, 2, 1, 3)
    return keep.reshape(R // TILE, C // TILE)


def draw_block_order(key, part):
    key = jax.random.fold_in(key, 5)
    key_middle, key_order = jax.random.split(key, 2)
    blocks = C // BLK
    middle = jax.random.permutation(key_middle, blocks - 2)[:NBLK - 2] + 1
    chosen = jnp.concatenate([jnp.array([0, blocks - 1], dtype=jnp.int32), middle.astype(jnp.int32)])
    order = jax.random.permutation(key_order, NBLK)
    return chosen[order].astype(jnp.int32)


def block_levels(key, extent, pieces, smallest, top_value):
    factor_of = 1.0
    for dim, blocks in pieces:
        draws = jax.random.uniform(jax.random.fold_in(jax.random.fold_in(key, 6), dim), (blocks,), jnp.float32, smallest / len(pieces), top_value / len(pieces))
        factor_of = factor_of * jnp.repeat(jnp.exp(draws), extent[dim] // blocks).reshape((-1,) + (1,) * (len(extent) - 1 - dim))
    return factor_of


def bell_draw(stream_key, shape, scale, bound, shards=(), held_as=jnp.bfloat16):
    result = jax.random.normal(stream_key, shape, jnp.float32) * scale
    if len(shards) > 0:
        result = block_levels(stream_key, shape, shards, -0.22, 0.18) * result
    return jnp.clip(result, min=-bound, max=bound).astype(held_as)


def setup_inputs(seed: int = 0) -> dict:
    key_list = jax.random.split(jax.random.key(seed), 6)
    weight = bell_draw(key_list[0], (R, C), 1.0, 6.0, ((0, 16), (1, 32)), jnp.float32)
    keep_tiles = draw_keep_tiles(jax.random.fold_in(key_list[5], 71), 0)
    factor_rows = bell_draw(key_list[2], (NBLK, BLK, C), BLK ** -0.5, 0.375, ((1, 16), (2, 32)), jnp.float32)
    diag_inverse = jnp.clip(jnp.exp(math.log(2.0) - 1.3862944 * jax.random.uniform(key_list[3], (C,), jnp.float32) ** block_levels(key_list[3], (C,), ((0, 32),), -0.2, 0.2)), 0.5, 2.0)
    block_order = draw_block_order(jax.random.fold_in(key_list[5], 71), 0)
    return {"weight": weight, "keep_tiles": keep_tiles, "factor_rows": factor_rows, "diag_inverse": diag_inverse, "block_order": block_order}


def reference(weight, keep_tiles, factor_rows, diag_inverse, block_order):
    current = weight
    col_block = jnp.arange(C, dtype=jnp.int32) // BLK
    for step in range(NBLK):
        start = (block_order[step] * BLK).astype(jnp.int32)
        block_w = lax.dynamic_slice_in_dim(current, start, BLK, 1)
        tiles = lax.dynamic_slice_in_dim(keep_tiles, (start // TILE).astype(jnp.int32), BLK // TILE, 1)
        block_keep = jnp.repeat(jnp.repeat(tiles, TILE, 0), TILE, 1).astype(jnp.float32)
        scales = lax.dynamic_slice_in_dim(diag_inverse, start, BLK, 0)
        errors = block_w * (1.0 - block_keep) * scales[None, :]
        update = jnp.dot(errors, factor_rows[step], preferred_element_type=jnp.float32, precision=lax.Precision.HIGHEST)
        finished = jnp.any(col_block[:, None] == block_order[None, :step + 1], axis=1)
        current = current - jnp.where(finished[None, :], jnp.float32(0.0), update)
    keep = jnp.repeat(jnp.repeat(keep_tiles, TILE, 0), TILE, 1).astype(jnp.float32)
    processed = jnp.any(col_block[:, None] == block_order[None, :], axis=1)
    return jnp.where(processed[None, :], current * keep, current)
```

```python
import jax
import jax.numpy as jnp
from jax import lax
from jax.experimental import pallas as pl
from jax.experimental.pallas import tpu as pltpu
from jax.sharding import PartitionSpec as P

MESH = pl.DeviceIdType.MESH
TILE = 128
NBLK = 4
MAXP = 10
NZ, NX, NY = 8, 4, 8
NIN, NOUT = NZ * NX, NY * 2
ROWS = MAXP * TILE
CH = ROWS // NIN
PAIRS = [(j, k) for k in range(NBLK) for j in range(k)]
GROWS = len(PAIRS) * 4
F32 = jnp.float32
NEAR = (1, 7, 2, 6, 3, 5, 4)


def wait_for(ref, sem):
    pltpu.make_async_copy(ref, ref, sem).wait()


def stage(bo_ref, keep_ref, w_hbm, f_ref, d_ref, m_out, ce_out, gc_ref, wb, sem):
    me = lax.axis_index("in")
    last = NIN - 1
    blk = 2 * TILE
    first_b, last_b = 0, 2 * NIN - 1
    bo = [bo_ref[k] for k in range(NBLK)]
    mid = [jnp.int32(0), jnp.int32(0)]
    seen = jnp.int32(0)
    for k in range(NBLK):
        is_mid = jnp.logical_and(bo[k] != first_b, bo[k] != last_b)
        for q in range(2):
            mid[q] = jnp.where(jnp.logical_and(is_mid, seen == q), bo[k], mid[q])
        seen = seen + is_mid.astype(jnp.int32)
    is_root = jnp.logical_or(me == 0, me == last)
    jobs = [
        (mid[0] // 2 == me, mid[0] % 2, m_out.at[0]),
        (mid[1] // 2 == me, mid[1] % 2, m_out.at[1]),
        (is_root, jnp.where(me == last, 1, 0), ce_out),
    ]

    def fetch(i):
        half = pl.ds(pl.multiple_of(jobs[i][1] * blk, blk), blk)
        return pltpu.make_async_copy(w_hbm.at[:, half], wb.at[i], sem.at[i])

    for i, (own, lb, out) in enumerate(jobs):
        @pl.when(own)
        def _():
            fetch(i).start()

    gc_ref[pl.ds(GROWS, NIN - GROWS)] = jnp.zeros((NIN - GROWS, 8, TILE), F32)
    row = lax.broadcasted_iota(jnp.int32, (8, TILE), 0)
    lane = lax.broadcasted_iota(jnp.int32, (8, TILE), 1)
    for k in range(NBLK):
        own = bo[k] // 2 == me

        @pl.when(own)
        def _():
            off = pl.multiple_of((bo[k] % 2) * blk, blk)
            cb = (bo[k] % 2) * 2
            flags = jnp.zeros((8, TILE), F32)
            for tt in range(16):
                pr = (1 - keep_ref[cb + tt % 2, tt // 2]).astype(F32)
                flags = jnp.where(jnp.logical_and(row == k, lane == tt), pr, flags)
            gc_ref[GROWS] = gc_ref[GROWS] + flags
            for half in range(2):
                d = d_ref[0:1, pl.ds(pl.multiple_of(off + half * TILE, TILE), TILE)]
                gc_ref[GROWS + 1, pl.ds(2 * k + half, 1), :] = d

        for p, (j, kk) in enumerate(PAIRS):
            if kk != k:
                continue

            @pl.when(own)
            def _():
                for half in range(2):
                    cols = pl.ds(pl.multiple_of((bo[k] % 2) * blk + half * TILE, TILE), TILE)
                    d = d_ref[0:1, cols]
                    for rh in range(2):
                        gc_ref[p * 4 + half * 2 + rh] = f_ref[j, pl.ds(rh * 8, 8), cols] * d

            @pl.when(jnp.logical_not(own))
            def _():
                gc_ref[pl.ds(p * 4, 4)] = jnp.zeros((4, 8, TILE), F32)

    for i, (own, lb, out) in enumerate(jobs):
        if i < 2:
            out[...] = jnp.zeros((ROWS, TILE), F32)

        @pl.when(own)
        def _():
            if i == 2:
                out[...] = jnp.zeros((ROWS, TILE), F32)
            fetch(i).wait()
            cnt = jnp.int32(0)
            for tt in range(16):
                r, cc = tt // 2, tt % 2
                pr = 1 - keep_ref[lb * 2 + cc, r]

                @pl.when(pr == 1)
                def _():
                    rows = pl.ds(pl.multiple_of(cnt * TILE, TILE), TILE)
                    out[rows, :] = wb[i, r * TILE : (r + 1) * TILE, cc * TILE : (cc + 1) * TILE]

                cnt = jnp.minimum(cnt + pr, MAXP - 1 if tt == 15 else MAXP)


def exchange(m, ce, gc_hbm, f_hbm, t_out, f_out, g_out, fl_out,
             t, mq, gc, rb1, sb2, rb2, grb, gf,
             loc, fl_sem, out_sem, f_s, f_r, fc_s, fc_r, g_s, g_r, gc_s, gc_r, grs_s, grs_r, gag_s, gag_r,
             sc_s, sc_r, r1_s, r1_r, r2_s, r2_r, a1e_s, a1e_r, a2e_s, a2e_r, a1m_s, a1m_r, a2m_s, a2m_r):
    o = lax.axis_index("out")
    me = lax.axis_index("in")
    y, c = o // 2, o % 2
    z, x = me // NX, me % NX
    last = NIN - 1
    is_root = jnp.logical_or(me == 0, me == last)

    gcopy = pltpu.make_async_copy(gc_hbm, gc, loc.at[0])
    gcopy.start()
    mcopy = pltpu.make_async_copy(m.at[:, :, pl.ds(pl.multiple_of(x * CH, 8), CH)], mq, loc.at[1])
    mcopy.start()
    fown = pltpu.make_async_copy(f_hbm, f_out.at[o], loc.at[2])
    fown.start()

    def ydev(dy):
        return (lax.rem(y + dy, NY) * 2 + c, me)

    def zdev(dz):
        return (o, lax.rem(z + dz, NZ) * NX + x)

    def xdev(dx):
        return (o, z * NX + lax.rem(x + dx, NX))

    other = (y * 2 + 1 - c, me)

    def send(src, dst, ssem, rsem, dev):
        pltpu.make_async_remote_copy(
            src_ref=src, dst_ref=dst, send_sem=ssem, recv_sem=rsem, device_id=dev, device_id_type=MESH
        ).start()

    barrier = pltpu.get_barrier_semaphore()

    def greet(r, _):
        pl.semaphore_signal(barrier, inc=1, device_id=(o, lax.rem(me + r, NIN)), device_id_type=MESH)
        return 0

    lax.fori_loop(1, NIN, greet, 0)
    for dy in range(1, NY):
        pl.semaphore_signal(barrier, inc=1, device_id=ydev(dy), device_id_type=MESH)
    pl.semaphore_signal(barrier, inc=1, device_id=other, device_id_type=MESH)
    pl.semaphore_wait(barrier, NIN - 1 + NY - 1 + 1)

    gcopy.wait()

    def spread_g(r, _):
        peer = lax.rem(me + r, NIN)
        send(gc.at[peer], grb.at[r], grs_s, grs_r, (o, peer))
        return 0

    lax.fori_loop(1, NIN, spread_g, 0)

    for dz in NEAR + (0,):
        for dx in range(1, NX):
            part = pl.ds(pl.multiple_of(lax.rem(x + dx, NX) * CH, 8), CH)
            send(m.at[:, lax.rem(z + dz, NZ), part], rb1.at[dz, dx - 1], r1_s, r1_r.at[dz], xdev(dx))

    for e in range(2):
        root = e * last

        @pl.when(me == root)
        def _():
            def scatter(r, _):
                peer = lax.rem(me + r, NIN)
                rows = pl.ds(pl.multiple_of(peer * CH, 8), CH)
                send(ce.at[rows], t.at[e, rows], sc_s, sc_r.at[e], (o, peer))
                return 0

            lax.fori_loop(1, NIN, scatter, 0)

    for dy in NEAR:
        send(f_hbm, f_out.at[o], f_s, f_r.at[dy - 1], ydev(dy))
    send(f_hbm, f_out.at[o], fc_s, fc_r, other)

    mine = pl.ds(pl.multiple_of(me * CH, 8), CH)

    wait_for(grb.at[pl.ds(1, NIN - 1)], grs_r)
    grb[0] = gc[me]
    gf[me] = jnp.sum(grb[...], axis=0)

    def back_g(r, _):
        send(gf.at[me], gf.at[me], gag_s, gag_r, (o, lax.rem(me + r, NIN)))
        return 0

    lax.fori_loop(1, NIN, back_g, 0)

    for e in range(2):
        root = e * last

        @pl.when(me == root)
        def _():
            own = pltpu.make_async_copy(ce.at[mine], t.at[e, mine], loc.at[4])
            own.start()
            own.wait()

        @pl.when(me != root)
        def _():
            wait_for(t.at[e, mine], sc_r.at[e])

    for dz in NEAR:
        send(t.at[pl.ds(0, 2), mine], t.at[pl.ds(0, 2), mine], a1e_s, a1e_r.at[dz - 1], zdev(dz))
    for dx in range(1, NX):
        send(t.at[pl.ds(0, 2), mine], t.at[pl.ds(0, 2), mine], a2e_s, a2e_r, xdev(dx))

    mcopy.wait()
    for dz in NEAR + (0,):
        wait_for(rb1.at[dz], r1_r.at[dz])
        acc = mq[:, lax.rem(z + dz, NZ)]
        for q in range(NX - 1):
            acc = acc + rb1[dz, q]
        sb2[dz] = acc
        if dz:
            send(sb2.at[dz], rb2.at[dz - 1], r2_s, r2_r, zdev(dz))

    for dz in NEAR:
        h = lax.rem(z + NZ - dz, NZ) * NX + x
        rows = pl.ds(pl.multiple_of(h * CH, 8), CH)
        wait_for(t.at[pl.ds(0, 2), rows], a1e_r.at[dz - 1])
        for dx in range(1, NX):
            send(t.at[pl.ds(0, 2), rows], t.at[pl.ds(0, 2), rows], a2e_s, a2e_r, xdev(dx))

    wait_for(gf.at[pl.ds(1, NIN - 1)], gag_r)
    gown = pltpu.make_async_copy(gf.at[pl.ds(0, GROWS)], g_out.at[o], loc.at[3])
    gown.start()
    flc = pltpu.make_async_copy(gf.at[pl.ds(GROWS, 2)], fl_out, fl_sem)
    flc.start()
    for dy in NEAR:
        send(gf.at[pl.ds(0, GROWS)], g_out.at[o], g_s, g_r.at[dy - 1], ydev(dy))
    send(gf.at[pl.ds(0, GROWS)], g_out.at[o], gc_s, gc_r, other)

    wait_for(rb2, r2_r)
    t[2:4, mine, :] = sb2[0] + jnp.sum(rb2[...], axis=0)
    for dz in NEAR:
        send(t.at[pl.ds(2, 2), mine], t.at[pl.ds(2, 2), mine], a1m_s, a1m_r.at[dz - 1], zdev(dz))
    for dx in range(1, NX):
        send(t.at[pl.ds(2, 2), mine], t.at[pl.ds(2, 2), mine], a2m_s, a2m_r, xdev(dx))

    for dy in NEAR:
        slot = lax.rem(y + NY - dy, NY) * 2 + c
        wait_for(f_out.at[slot], f_r.at[dy - 1])
        send(f_out.at[slot], f_out.at[slot], fc_s, fc_r, other)

    for dz in NEAR:
        h = lax.rem(z + NZ - dz, NZ) * NX + x
        rows = pl.ds(pl.multiple_of(h * CH, 8), CH)
        wait_for(t.at[pl.ds(2, 2), rows], a1m_r.at[dz - 1])
        for dx in range(1, NX):
            send(t.at[pl.ds(2, 2), rows], t.at[pl.ds(2, 2), rows], a2m_s, a2m_r, xdev(dx))

    some = pl.ds(0, (NX - 1) * NZ * CH)
    wait_for(t.at[pl.ds(0, 2), some], a2e_r)
    ends_out = pltpu.make_async_copy(t.at[pl.ds(0, 2)], t_out.at[pl.ds(0, 2)], out_sem.at[0])
    ends_out.start()

    for dy in NEAR:
        slot = lax.rem(y + NY - dy, NY) * 2 + c
        wait_for(g_out.at[slot], g_r.at[dy - 1])
        send(g_out.at[slot], g_out.at[slot], gc_s, gc_r, other)

    wait_for(t.at[pl.ds(2, 2), some], a2m_r)
    mids_out = pltpu.make_async_copy(t.at[pl.ds(2, 2)], t_out.at[pl.ds(2, 2)], out_sem.at[1])
    mids_out.start()
    wait_for(f_out.at[pl.ds(0, NY)], fc_r)
    wait_for(g_out.at[pl.ds(0, NY)], gc_r)

    fown.wait()
    gown.wait()
    flc.wait()
    wait_for(f_out.at[pl.ds(0, NY - 1)], f_s)
    wait_for(f_out.at[pl.ds(0, NY)], fc_s)
    wait_for(g_out.at[pl.ds(0, NY - 1)], g_s)
    wait_for(g_out.at[pl.ds(0, NY)], gc_s)
    wait_for(grb.at[pl.ds(1, NIN - 1)], grs_s)
    wait_for(grb.at[pl.ds(1, NIN - 1)], gag_s)
    wait_for(rb1.at[:], r1_s)
    wait_for(rb2, r2_s)
    for s in (a1e_s, a1m_s):
        wait_for(t.at[pl.ds(0, 2), pl.ds(0, (NZ - 1) * CH)], s)
    for s in (a2e_s, a2m_s):
        wait_for(t.at[pl.ds(0, 2), some], s)

    @pl.when(is_root)
    def _():
        wait_for(ce.at[pl.ds(CH, (NIN - 1) * CH)], sc_s)

    ends_out.wait()
    mids_out.wait()


def split(v):
    hi = v.astype(jnp.bfloat16)
    return hi, (v - hi.astype(F32)).astype(jnp.bfloat16)


def dot3(ah, al, bh, bl):
    dot = lambda a, b: jnp.dot(a, b, preferred_element_type=F32)
    return dot(ah, bh) + (dot(ah, bl) + dot(al, bh))


def compensate(rt, bo_ref, keep_ref, fl_ref, dv_ref, t_ref, f_ref, g_ref, w_ref, o_ref, fh, flo, gh, glo, eh, elo):
    i = pl.program_id(0)
    me = lax.axis_index("in")
    blk = 2 * TILE
    bo = [bo_ref[k] for k in range(NBLK)]

    @pl.when(i == 0)
    def _():
        for k in range(NBLK):
            for lb in range(2):
                b = me * 2 + lb
                done = bo[0] == b
                for j in range(1, k + 1):
                    done = jnp.logical_or(done, bo[j] == b)
                v = f_ref[:, k, :, pl.ds(lb * blk, blk)].reshape(blk, blk)
                hi, lo = split(jnp.where(done, 0.0, v))
                fh[pl.ds(k * blk, blk), pl.ds(lb * blk, blk)] = hi
                flo[pl.ds(k * blk, blk), pl.ds(lb * blk, blk)] = lo
        for p in range(len(PAIRS)):
            for half in range(2):
                v = g_ref[:, pl.ds(p * 4 + half * 2, 2)].reshape(blk, TILE)
                hi, lo = split(v)
                gh[p, :, pl.ds(half * TILE, TILE)] = hi
                glo[p, :, pl.ds(half * TILE, TILE)] = lo

    seen = jnp.int32(0)
    for k in range(NBLK):
        is_first, is_last = bo[k] == 0, bo[k] == 2 * NIN - 1
        src = jnp.where(is_first, 0, jnp.where(is_last, 1, 2 + seen))
        seen = seen + jnp.where(jnp.logical_or(is_first, is_last), 0, 1)
        acc = None
        for j in range(k):
            p = PAIRS.index((j, k))
            part = dot3(eh[:, pl.ds(j * blk, blk)], elo[:, pl.ds(j * blk, blk)], gh[p], glo[p])
            acc = part if acc is None else acc + part
        base = jnp.int32(0)
        for tt in range(16):
            base = base + jnp.where(jnp.logical_and(tt < i * rt * 2, fl_ref[0, k, tt] > 0.5), 1, 0)
        for r in range(rt):
            for cc in range(2):
                on = fl_ref[0, k, (i * rt + r) * 2 + cc] > 0.5
                rows = pl.ds(pl.multiple_of(jnp.where(on, base, 0) * TILE, TILE), TILE)
                v = t_ref[src, rows, :] * dv_ref[1, 2 * k + cc : 2 * k + cc + 1, :]
                if acc is not None:
                    v = v - acc[r * TILE : (r + 1) * TILE, cc * TILE : (cc + 1) * TILE]
                hi, lo = split(jnp.where(on, v, 0.0))
                at = (pl.ds(r * TILE, TILE), pl.ds(k * blk + cc * TILE, TILE))
                eh[at] = hi
                elo[at] = lo
                base = base + jnp.where(on, 1, 0)

    upd = dot3(eh[...], elo[...], fh[...], flo[...])
    for cc in range(4):
        b = me * 2 + cc // 2
        done = bo[0] == b
        for j in range(1, NBLK):
            done = jnp.logical_or(done, bo[j] == b)
        for r in range(rt):
            kept = jnp.where(done, keep_ref[cc, i * rt + r], 1).astype(F32)
            at = (slice(r * TILE, (r + 1) * TILE), slice(cc * TILE, (cc + 1) * TILE))
            o_ref[at] = (w_ref[at] - upd[at]) * kept


def body(weight, keep_tiles, factor_rows, diag_inverse, block_order):
    rows, cols = weight.shape
    fshape = factor_rows.shape
    smem = pl.BlockSpec(memory_space=pltpu.SMEM)
    vmem = pl.BlockSpec(memory_space=pltpu.VMEM)
    anym = pl.BlockSpec(memory_space=pl.ANY)
    dma = pltpu.SemaphoreType.DMA
    one = dma(())
    mids, ends, shares = pl.pallas_call(
        stage,
        out_shape=(
            jax.ShapeDtypeStruct((2, ROWS, TILE), F32),
            jax.ShapeDtypeStruct((ROWS, TILE), F32),
            jax.ShapeDtypeStruct((NIN, 8, TILE), F32),
        ),
        in_specs=[smem, smem, anym, vmem, vmem],
        out_specs=(vmem, vmem, vmem),
        scratch_shapes=[pltpu.VMEM((3, rows, 2 * TILE), F32), dma((3,))],
        compiler_params=pltpu.CompilerParams(vmem_limit_bytes=12 << 20),
    )(block_order, keep_tiles.T, weight, factor_rows, diag_inverse.reshape(1, cols))
    tiles, facs, pans, flags = pl.pallas_call(
        exchange,
        out_shape=(
            jax.ShapeDtypeStruct((NBLK, ROWS, TILE), F32),
            jax.ShapeDtypeStruct((NOUT,) + fshape, F32),
            jax.ShapeDtypeStruct((NOUT, GROWS, 8, TILE), F32),
            jax.ShapeDtypeStruct((2, 8, TILE), F32),
        ),
        in_specs=[anym, anym, anym, anym],
        out_specs=(anym, anym, anym, anym),
        scratch_shapes=[
            pltpu.VMEM((NBLK, ROWS, TILE), F32),
            pltpu.VMEM((2, NZ, CH, TILE), F32),
            pltpu.VMEM((NIN, 8, TILE), F32),
            pltpu.VMEM((NZ, NX - 1, 2, CH, TILE), F32),
            pltpu.VMEM((NZ, 2, CH, TILE), F32),
            pltpu.VMEM((NZ - 1, 2, CH, TILE), F32),
            pltpu.VMEM((NIN, 8, TILE), F32),
            pltpu.VMEM((NIN, 8, TILE), F32),
            dma((5,)), one, dma((2,)),
            one, dma((NY - 1,)), one, one,
            one, dma((NY - 1,)), one, one,
            one, one, one, one,
            one, dma((2,)), one, dma((NZ,)), one, one,
            one, dma((NZ - 1,)), one, one,
            one, dma((NZ - 1,)), one, one,
        ],
        compiler_params=pltpu.CompilerParams(
            collective_id=0, has_side_effects=True, vmem_limit_bytes=16 << 20
        ),
    )(mids.reshape(2, NZ, NX * CH, TILE), ends, shares, factor_rows)

    rt = 4
    br = rt * TILE
    depth = NBLK * 2 * TILE
    return pl.pallas_call(
        lambda *refs: compensate(rt, *refs),
        grid=(rows // br,),
        out_shape=jax.ShapeDtypeStruct((rows, cols), F32),
        in_specs=[
            smem, smem, smem, vmem, vmem, vmem, vmem,
            pl.BlockSpec((br, cols), lambda i: (i, 0)),
        ],
        out_specs=pl.BlockSpec((br, cols), lambda i: (i, 0)),
        scratch_shapes=[
            pltpu.VMEM((depth, cols), jnp.bfloat16),
            pltpu.VMEM((depth, cols), jnp.bfloat16),
            pltpu.VMEM((len(PAIRS), 2 * TILE, 2 * TILE), jnp.bfloat16),
            pltpu.VMEM((len(PAIRS), 2 * TILE, 2 * TILE), jnp.bfloat16),
            pltpu.VMEM((br, depth), jnp.bfloat16),
            pltpu.VMEM((br, depth), jnp.bfloat16),
        ],
        compiler_params=pltpu.CompilerParams(vmem_limit_bytes=32 << 20),
    )(block_order, keep_tiles.T, flags, flags, tiles, facs, pans, weight)


def solution(mesh):
    return jax.shard_map(
        body,
        mesh=mesh,
        in_specs=(P("out", "in"), P("out", "in"), P(None, "out", "in"), P("in"), P()),
        out_specs=P("out", "in"),
        check_vma=False,
    )
```

```python
import jax
import jax.numpy as jnp
from jax import lax
from jax.experimental import pallas as pl
from jax.experimental.pallas import tpu as pltpu
from jax.sharding import PartitionSpec as P

MESH = pl.DeviceIdType.MESH
TILE = 128
NBLK = 4
MAXP = 10
NZ, NX, NY = 8, 4, 8
NIN, NOUT = NZ * NX, NY * 2
ROWS = MAXP * TILE
CH = ROWS // NIN
PAIRS = [(j, k) for k in range(NBLK) for j in range(k)]
GROWS = len(PAIRS) * 4
F32 = jnp.float32
NEAR = (1, 7, 2, 6, 3, 5, 4)
FAR = (4, 3, 5, 2, 6, 1, 7)


def wait_for(ref, sem):
    pltpu.make_async_copy(ref, ref, sem).wait()


def stage(bo_hbm, keep_hbm, w_hbm, f_hbm, d_hbm, m_out, ce_out, gc_ref, bo_ref, keep_ref, w, f_ref, d_ref, sem):
    moves = [
        pltpu.make_async_copy(src, dst, sem.at[i])
        for i, (src, dst) in enumerate(
            ((bo_hbm, bo_ref), (keep_hbm, keep_ref), (d_hbm, d_ref), (f_hbm, f_ref), (w_hbm, w))
        )
    ]
    for move in moves:
        move.start()
    me = lax.axis_index("in")
    last = NIN - 1
    blk = 2 * TILE
    m_out[...] = jnp.zeros_like(m_out)
    gc_ref[...] = jnp.zeros_like(gc_ref)
    for move in moves[:4]:
        move.wait()
    first_b, last_b = 0, 2 * NIN - 1
    bo = [bo_ref[k] for k in range(NBLK)]
    mid = [jnp.int32(0), jnp.int32(0)]
    seen = jnp.int32(0)
    for k in range(NBLK):
        is_mid = jnp.logical_and(bo[k] != first_b, bo[k] != last_b)
        for q in range(2):
            mid[q] = jnp.where(jnp.logical_and(is_mid, seen == q), bo[k], mid[q])
        seen = seen + is_mid.astype(jnp.int32)
    is_root = jnp.logical_or(me == 0, me == last)
    jobs = [
        (mid[0] // 2 == me, mid[0] % 2, m_out.at[0]),
        (mid[1] // 2 == me, mid[1] % 2, m_out.at[1]),
        (is_root, jnp.where(me == last, 1, 0), ce_out),
    ]

    row = lax.broadcasted_iota(jnp.int32, (8, TILE), 0)
    lane = lax.broadcasted_iota(jnp.int32, (8, TILE), 1)
    for k in range(NBLK):
        own = bo[k] // 2 == me

        @pl.when(own)
        def _():
            off = pl.multiple_of((bo[k] % 2) * blk, blk)
            cb = (bo[k] % 2) * 2
            flags = jnp.zeros((8, TILE), F32)
            for tt in range(16):
                pr = (1 - keep_ref[cb + tt % 2, tt // 2]).astype(F32)
                flags = jnp.where(jnp.logical_and(row == k, lane == tt), pr, flags)
            gc_ref[GROWS] = gc_ref[GROWS] + flags
            for half in range(2):
                d = d_ref[0:1, pl.ds(pl.multiple_of(off + half * TILE, TILE), TILE)]
                gc_ref[GROWS + 1, pl.ds(2 * k + half, 1), :] = d

        for p, (j, kk) in enumerate(PAIRS):
            if kk != k:
                continue

            @pl.when(own)
            def _():
                for half in range(2):
                    cols = pl.ds(pl.multiple_of((bo[k] % 2) * blk + half * TILE, TILE), TILE)
                    d = d_ref[0:1, cols]
                    for rh in range(2):
                        gc_ref[p * 4 + half * 2 + rh] = f_ref[j, pl.ds(rh * 8, 8), cols] * d

    moves[4].wait()
    for i, (own, lb, out) in enumerate(jobs):

        @pl.when(own)
        def _():
            if i == 2:
                out[...] = jnp.zeros((ROWS, TILE), F32)
            base = pl.multiple_of(lb * blk, blk)
            cnt = jnp.int32(0)
            for tt in range(16):
                r, cc = tt // 2, tt % 2
                pr = 1 - keep_ref[lb * 2 + cc, r]

                @pl.when(pr == 1)
                def _():
                    rows = pl.ds(pl.multiple_of(cnt * TILE, TILE), TILE)
                    out[rows, :] = w[pl.ds(r * TILE, TILE), pl.ds(base + cc * TILE, TILE)]

                cnt = jnp.minimum(cnt + pr, MAXP - 1 if tt == 15 else MAXP)


def exchange(m, ce, gc_hbm, f_hbm, t_out, f_out, g_out, fl_out,
             om, mq, gc, rb1, sb2, rb2, grb, gf,
             loc, fl_sem, f_s, f_r, fc_s, fc_r, g_s, g_r, gc_s, gc_r, grs_s, grs_r, gag_s, gag_r,
             sc_s, sc_r, r1_s, r1_r, r2_s, r2_r, a1_s, a1_r, a2_s, a2_r, ex_s, ex_r, z_s, zp_r, zm_r, zl_r):
    o = lax.axis_index("out")
    me = lax.axis_index("in")
    y, c = o // 2, o % 2
    z, x = me // NX, me % NX
    last = NIN - 1
    is_root = jnp.logical_or(me == 0, me == last)

    gcopy = pltpu.make_async_copy(gc_hbm, gc, loc.at[0])
    gcopy.start()
    mcopy = pltpu.make_async_copy(m.at[:, :, pl.ds(pl.multiple_of(x * CH, 8), CH)], mq, loc.at[1])
    mcopy.start()
    fown = pltpu.make_async_copy(f_hbm, f_out.at[o], loc.at[2])
    fown.start()

    def ydev(dy):
        return (lax.rem(y + dy, NY) * 2 + c, me)

    def zdev(dz):
        return (o, lax.rem(z + dz, NZ) * NX + x)

    def xdev(dx):
        return (o, z * NX + lax.rem(x + dx, NX))

    other = (y * 2 + 1 - c, me)

    def send(src, dst, ssem, rsem, dev):
        pltpu.make_async_remote_copy(
            src_ref=src, dst_ref=dst, send_sem=ssem, recv_sem=rsem, device_id=dev, device_id_type=MESH
        ).start()

    barrier = pltpu.get_barrier_semaphore()

    def greet(r, _):
        pl.semaphore_signal(barrier, inc=1, device_id=(o, lax.rem(me + r, NIN)), device_id_type=MESH)
        return 0

    lax.fori_loop(1, NIN, greet, 0)
    for dy in range(1, NY):
        pl.semaphore_signal(barrier, inc=1, device_id=ydev(dy), device_id_type=MESH)
    pl.semaphore_signal(barrier, inc=1, device_id=other, device_id_type=MESH)
    pl.semaphore_wait(barrier, NIN - 1 + NY - 1 + 1)

    gcopy.wait()

    def spread_g(r, _):
        peer = lax.rem(me + r, NIN)
        send(gc.at[peer], grb.at[r], grs_s, grs_r, (o, peer))
        return 0

    lax.fori_loop(1, NIN, spread_g, 0)

    for dz in FAR + (0,):
        for dx in range(1, NX):
            part = pl.ds(pl.multiple_of(lax.rem(x + dx, NX) * CH, 8), CH)
            send(m.at[:, lax.rem(z + dz, NZ), part], rb1.at[dz, dx - 1], r1_s, r1_r.at[dz], xdev(dx))

    for e in range(2):
        root = e * last

        @pl.when(me == root)
        def _():
            def scatter(r, _):
                peer = lax.rem(me + r, NIN)
                rows = pl.ds(pl.multiple_of(peer * CH, 8), CH)
                send(ce.at[rows], t_out.at[e, rows], sc_s, sc_r.at[e], (o, peer))
                return 0

            lax.fori_loop(1, NIN, scatter, 0)

    def yslot(dst, dy):
        return dst.at[lax.rem(y + NY - dy, NY) * 2 + c]

    def y_start(src, dst, ssem, rsem, csem, crsem):
        for dy in (1, NY - 1, 2, NY - 2):
            send(src, dst.at[o], ssem, rsem.at[dy - 1], ydev(dy))
        send(src, dst.at[o], csem, crsem, other)

    def y_onward(dst, ssem, rsem, csem, crsem):
        for dy, hops in ((2, ((1, 3), (2, 4))), (NY - 2, ((NY - 1, NY - 3),))):
            src = yslot(dst, dy)
            wait_for(src, rsem.at[dy - 1])
            for hop, total in hops:
                send(src, src, ssem, rsem.at[total - 1], ydev(hop))
            send(src, src, csem, crsem, other)

    def y_finish(dst, rsem, csem, crsem):
        for dy in (1, NY - 1, 3, NY - 3, 4):
            src = yslot(dst, dy)
            wait_for(src, rsem.at[dy - 1])
            send(src, src, csem, crsem, other)

    y_start(f_hbm, f_out, f_s, f_r, fc_s, fc_r)

    def chunk(dz, dx):
        h = lax.rem(z + NZ - dz, NZ) * NX + lax.rem(x + NX - dx, NX)
        return pl.ds(pl.multiple_of(h * CH, 8), CH)

    mine = chunk(0, 0)

    pair = pl.ds(2, 2)

    def from_z(dz, src):
        dst = t_out.at[pair, chunk(dz, 0)]
        for dx in range(1, NX):
            send(src, dst, a2_s, a2_r, xdev(dx))

    def zrow(dz, e=pl.ds(0, 2)):
        return t_out.at[e, pl.ds(pl.multiple_of(lax.rem(z + NZ - dz, NZ) * NX * CH, 8), NX * CH)]

    def round_z(n):
        if n:
            wait_for(zrow(n), zp_r.at[n - 1])
            wait_for(zrow(NZ - n), zm_r.at[n - 1])
        if n < NZ // 2 - 1:
            send(zrow(n), zrow(n), z_s, zp_r.at[n], zdev(1))
            send(zrow(NZ - n), zrow(NZ - n), z_s, zm_r.at[n], zdev(NZ - 1))
        else:
            send(zrow(n, 0), zrow(n, 0), z_s, zl_r.at[0], zdev(1))
            send(zrow(NZ - n, 1), zrow(NZ - n, 1), z_s, zl_r.at[1], zdev(NZ - 1))

    wait_for(grb.at[pl.ds(1, NIN - 1)], grs_r)
    grb[0] = gc[me]
    gf[me] = jnp.sum(grb[...], axis=0)

    def back_g(r, _):
        send(gf.at[me], gf.at[me], gag_s, gag_r, (o, lax.rem(me + r, NIN)))
        return 0

    lax.fori_loop(1, NIN, back_g, 0)

    for e in range(2):
        root = e * last

        @pl.when(me == root)
        def _():
            own = pltpu.make_async_copy(ce.at[mine], t_out.at[e, mine], loc.at[4])
            own.start()
            own.wait()

        @pl.when(me != root)
        def _():
            wait_for(t_out.at[e, mine], sc_r.at[e])

    for dx in range(1, NX):
        send(t_out.at[pl.ds(0, 2), mine], t_out.at[pl.ds(0, 2), mine], ex_s, ex_r, xdev(dx))

    mcopy.wait()
    y_onward(f_out, f_s, f_r, fc_s, fc_r)

    for dz in FAR + (0,):
        wait_for(rb1.at[dz], r1_r.at[dz])
        acc = mq[:, lax.rem(z + dz, NZ)]
        for q in range(NX - 1):
            acc = acc + rb1[dz, q]
        sb2[dz] = acc
        if dz:
            send(sb2.at[dz], rb2.at[dz - 1], r2_s, r2_r, zdev(dz))

    wait_for(t_out.at[pl.ds(0, 2), pl.ds(0, (NX - 1) * CH)], ex_r)
    round_z(0)

    wait_for(gf.at[pl.ds(1, NIN - 1)], gag_r)
    gown = pltpu.make_async_copy(gf.at[pl.ds(0, GROWS)], g_out.at[o], loc.at[3])
    gown.start()
    flc = pltpu.make_async_copy(gf.at[pl.ds(GROWS, 2)], fl_out, fl_sem)
    flc.start()
    y_start(gf.at[pl.ds(0, GROWS)], g_out, g_s, g_r, gc_s, gc_r)

    wait_for(rb2, r2_r)
    om[...] = sb2[0] + jnp.sum(rb2[...], axis=0)
    for dz in FAR:
        send(om, t_out.at[pair, mine], a1_s, a1_r.at[dz - 1], zdev(dz))
    from_z(0, om)
    omc = pltpu.make_async_copy(om, t_out.at[pair, mine], loc.at[5])
    omc.start()
    round_z(1)
    y_finish(f_out, f_r, fc_s, fc_r)
    for n, dz in enumerate(NEAR):
        wait_for(t_out.at[pair, chunk(dz, 0)], a1_r.at[dz - 1])
        from_z(dz, t_out.at[pair, chunk(dz, 0)])
        if n == 2:
            round_z(2)
    y_onward(g_out, g_s, g_r, gc_s, gc_r)
    round_z(3)
    y_finish(g_out, g_r, gc_s, gc_r)

    wait_for(zrow(4, 0), zl_r.at[0])
    wait_for(zrow(4, 1), zl_r.at[1])
    wait_for(t_out.at[pair, pl.ds(0, 3 * NZ * CH)], a2_r)
    wait_for(f_out.at[pl.ds(0, NY)], fc_r)
    wait_for(g_out.at[pl.ds(0, NY)], gc_r)
    omc.wait()
    fown.wait()
    gown.wait()
    flc.wait()
    wait_for(f_out.at[pl.ds(0, NY - 1)], f_s)
    wait_for(f_out.at[pl.ds(0, NY)], fc_s)
    wait_for(g_out.at[pl.ds(0, NY - 1)], g_s)
    wait_for(g_out.at[pl.ds(0, NY)], gc_s)
    wait_for(grb.at[pl.ds(1, NIN - 1)], grs_s)
    wait_for(grb.at[pl.ds(1, NIN - 1)], gag_s)
    wait_for(rb1.at[:], r1_s)
    wait_for(rb2, r2_s)
    wait_for(t_out.at[pair, pl.ds(0, (NZ - 1) * CH)], a1_s)
    wait_for(t_out.at[pair, pl.ds(0, 3 * NZ * CH)], a2_s)
    wait_for(t_out.at[pl.ds(0, 2), pl.ds(0, (NX - 1) * CH)], ex_s)
    wait_for(t_out.at[pl.ds(0, 2), pl.ds(0, (NZ - 1) * NX * CH)], z_s)

    @pl.when(is_root)
    def _():
        wait_for(ce.at[pl.ds(CH, (NIN - 1) * CH)], sc_s)


def split(v):
    hi = v.astype(jnp.bfloat16)
    return hi, (v - hi.astype(F32)).astype(jnp.bfloat16)


def dot(a, b):
    return jnp.dot(a, b, preferred_element_type=F32)


def compensate(rt, bo_ref, keep_ref, fl_ref, dv_ref, t_ref, f_ref, g_ref, w_ref, o_hbm, f3, g3, e3, ob, start, osem):
    me = lax.axis_index("in")
    blk = 2 * TILE
    bo = [bo_ref[k] for k in range(NBLK)]

    for k in range(NBLK):
        for lb in range(2):
            b = me * 2 + lb
            done = bo[0] == b
            for j in range(1, k + 1):
                done = jnp.logical_or(done, bo[j] == b)
            v = f_ref[:, k, :, pl.ds(lb * blk, blk)].reshape(blk, blk)
            hi, lo = split(jnp.where(done, 0.0, v))
            for n, part in enumerate((hi, hi, lo)):
                f3[pl.ds((3 * k + n) * blk, blk), pl.ds(lb * blk, blk)] = part
    for p, (j, k) in enumerate(PAIRS):
        for half in range(2):
            v = g_ref[:, pl.ds(p * 4 + half * 2, 2)].reshape(blk, TILE)
            hi, lo = split(v)
            for n, part in enumerate((hi, hi, lo)):
                g3[k - 1, pl.ds((3 * j + n) * blk, blk), pl.ds(half * TILE, TILE)] = part

    srcs = []
    seen = jnp.int32(0)
    for k in range(NBLK):
        is_first, is_last = bo[k] == 0, bo[k] == 2 * NIN - 1
        srcs.append(jnp.where(is_first, 0, jnp.where(is_last, 1, 2 + seen)))
        seen = seen + jnp.where(jnp.logical_or(is_first, is_last), 0, 1)
        base = jnp.int32(0)
        for tt in range(16):
            on = fl_ref[0, k, tt] > 0.5
            start[k, tt] = jnp.where(on, base, -1)
            base = base + jnp.where(on, TILE, 0)

    nb = w_ref.shape[0] // (rt * TILE)
    br = rt * TILE
    for k in range(NBLK):
        for i in range(nb):
            acc = dot(e3[pl.ds(i * br, br), : 3 * k * blk], g3[k - 1, : 3 * k * blk]) if k else None
            for r in range(rt):
                for cc in range(2):
                    base = start[k, (i * rt + r) * 2 + cc]
                    rows = pl.ds(pl.multiple_of(jnp.maximum(base, 0), TILE), TILE)
                    v = t_ref[srcs[k], rows, :] * dv_ref[1, 2 * k + cc : 2 * k + cc + 1, :]
                    if acc is not None:
                        v = v - acc[r * TILE : (r + 1) * TILE, cc * TILE : (cc + 1) * TILE]
                    hi, lo = split(jnp.where(base >= 0, v, 0.0))
                    for n, part in enumerate((hi, lo, hi)):
                        e3[pl.ds(i * br + r * TILE, TILE), pl.ds((3 * k + n) * blk + cc * TILE, TILE)] = part

    copies = []
    for i in range(nb):
        upd = dot(e3[pl.ds(i * br, br), :], f3[...])
        for cc in range(4):
            b = me * 2 + cc // 2
            done = bo[0] == b
            for j in range(1, NBLK):
                done = jnp.logical_or(done, bo[j] == b)
            for r in range(rt):
                kept = jnp.where(done, keep_ref[cc, i * rt + r], 1).astype(F32)
                at = (pl.ds(i * br + r * TILE, TILE), pl.ds(cc * TILE, TILE))
                ob[at] = (w_ref[at] - upd[r * TILE : (r + 1) * TILE, cc * TILE : (cc + 1) * TILE]) * kept
        rows = pl.ds(i * br, br)
        copies.append(pltpu.make_async_copy(ob.at[rows], o_hbm.at[rows], osem.at[i]))
        copies[-1].start()
    for copy in copies:
        copy.wait()


def body(weight, keep_tiles, factor_rows, diag_inverse, block_order):
    rows, cols = weight.shape
    fshape = factor_rows.shape
    smem = pl.BlockSpec(memory_space=pltpu.SMEM)
    vmem = pl.BlockSpec(memory_space=pltpu.VMEM)
    anym = pl.BlockSpec(memory_space=pl.ANY)
    hbm = pl.BlockSpec(memory_space=pltpu.HBM)
    dma = pltpu.SemaphoreType.DMA
    one = dma(())
    mids, ends, shares = pl.pallas_call(
        stage,
        out_shape=(
            jax.ShapeDtypeStruct((2, ROWS, TILE), F32),
            jax.ShapeDtypeStruct((ROWS, TILE), F32),
            jax.ShapeDtypeStruct((NIN, 8, TILE), F32),
        ),
        in_specs=[hbm] * 5,
        out_specs=(vmem, vmem, vmem),
        scratch_shapes=[
            pltpu.SMEM(block_order.shape, jnp.int32),
            pltpu.SMEM(keep_tiles.T.shape, jnp.int32),
            pltpu.VMEM((rows, cols), F32),
            pltpu.VMEM(fshape, F32),
            pltpu.VMEM((1, cols), F32),
            dma((5,)),
        ],
        compiler_params=pltpu.CompilerParams(vmem_limit_bytes=12 << 20),
    )(block_order, keep_tiles.T, weight, factor_rows, diag_inverse.reshape(1, cols))
    tiles, facs, pans, flags = pl.pallas_call(
        exchange,
        out_shape=(
            jax.ShapeDtypeStruct((NBLK, ROWS, TILE), F32),
            jax.ShapeDtypeStruct((NOUT,) + fshape, F32),
            jax.ShapeDtypeStruct((NOUT, GROWS, 8, TILE), F32),
            jax.ShapeDtypeStruct((2, 8, TILE), F32),
        ),
        in_specs=[anym, anym, anym, anym],
        out_specs=(anym, anym, anym, anym),
        scratch_shapes=[
            pltpu.VMEM((2, CH, TILE), F32),
            pltpu.VMEM((2, NZ, CH, TILE), F32),
            pltpu.VMEM((NIN, 8, TILE), F32),
            pltpu.VMEM((NZ, NX - 1, 2, CH, TILE), F32),
            pltpu.VMEM((NZ, 2, CH, TILE), F32),
            pltpu.VMEM((NZ - 1, 2, CH, TILE), F32),
            pltpu.VMEM((NIN, 8, TILE), F32),
            pltpu.VMEM((NIN, 8, TILE), F32),
            dma((6,)), one,
            one, dma((NY - 1,)), one, one,
            one, dma((NY - 1,)), one, one,
            one, one, one, one,
            one, dma((2,)), one, dma((NZ,)), one, one,
            one, dma((NZ - 1,)), one, one, one, one, one, dma((3,)), dma((3,)), dma((2,)),
        ],
        compiler_params=pltpu.CompilerParams(
            collective_id=0, has_side_effects=True, vmem_limit_bytes=16 << 20
        ),
    )(mids.reshape(2, NZ, NX * CH, TILE), ends, shares, factor_rows)

    rt = 4
    br = rt * TILE
    depth = NBLK * 2 * TILE
    bf16 = jnp.bfloat16
    return pl.pallas_call(
        lambda *refs: compensate(rt, *refs),
        out_shape=jax.ShapeDtypeStruct((rows, cols), F32),
        in_specs=[smem, smem, smem, vmem, vmem, vmem, vmem, vmem],
        out_specs=anym,
        scratch_shapes=[
            pltpu.VMEM((3 * depth, cols), bf16),
            pltpu.VMEM((NBLK - 1, 3 * (NBLK - 1) * 2 * TILE, 2 * TILE), bf16),
            pltpu.VMEM((rows, 3 * depth), bf16),
            pltpu.VMEM((rows, cols), F32),
            pltpu.SMEM((NBLK, 16), jnp.int32),
            dma((rows // br,)),
        ],
        compiler_params=pltpu.CompilerParams(vmem_limit_bytes=24 << 20),
    )(block_order, keep_tiles.T, flags, flags, tiles, facs, pans, weight)


def solution(mesh):
    return jax.shard_map(
        body,
        mesh=mesh,
        in_specs=(P("out", "in"), P("out", "in"), P(None, "out", "in"), P("in"), P()),
        out_specs=P("out", "in"),
        check_vma=False,
    )
```

```python
import jax
import jax.numpy as jnp
from jax import lax
from jax.experimental import pallas as pl
from jax.experimental.pallas import tpu as pltpu
from jax.sharding import PartitionSpec as P

MESH = pl.DeviceIdType.MESH
TILE = 128
NBLK = 4
MAXP = 10
NZ, NX, NY = 8, 4, 8
NIN, NOUT = NZ * NX, NY * 2
ROWS = MAXP * TILE
CH = ROWS // NIN
PAIRS = [(j, k) for k in range(NBLK) for j in range(k)]
GROWS = len(PAIRS) * 4
F32 = jnp.float32
NEAR = (1, 7, 2, 6, 3, 5, 4)
FAR = (4, 3, 5, 2, 6, 1, 7)


def wait_for(ref, sem):
    pltpu.make_async_copy(ref, ref, sem).wait()


def stage(bo_hbm, keep_hbm, w_hbm, f_hbm, d_hbm, m_out, ce_out, gc_ref, bo_ref, keep_ref, w, f_ref, d_ref, sem):
    moves = [
        pltpu.make_async_copy(src, dst, sem.at[i])
        for i, (src, dst) in enumerate(
            ((bo_hbm, bo_ref), (keep_hbm, keep_ref), (d_hbm, d_ref), (f_hbm, f_ref), (w_hbm, w))
        )
    ]
    for move in moves:
        move.start()
    me = lax.axis_index("in")
    last = NIN - 1
    blk = 2 * TILE
    m_out[...] = jnp.zeros_like(m_out)
    gc_ref[...] = jnp.zeros_like(gc_ref)
    for move in moves[:4]:
        move.wait()
    first_b, last_b = 0, 2 * NIN - 1
    bo = [bo_ref[k] for k in range(NBLK)]
    mid = [jnp.int32(0), jnp.int32(0)]
    seen = jnp.int32(0)
    for k in range(NBLK):
        is_mid = jnp.logical_and(bo[k] != first_b, bo[k] != last_b)
        for q in range(2):
            mid[q] = jnp.where(jnp.logical_and(is_mid, seen == q), bo[k], mid[q])
        seen = seen + is_mid.astype(jnp.int32)
    is_root = jnp.logical_or(me == 0, me == last)
    jobs = [
        (mid[0] // 2 == me, mid[0] % 2, m_out.at[0]),
        (mid[1] // 2 == me, mid[1] % 2, m_out.at[1]),
        (is_root, jnp.where(me == last, 1, 0), ce_out),
    ]

    row = lax.broadcasted_iota(jnp.int32, (8, TILE), 0)
    lane = lax.broadcasted_iota(jnp.int32, (8, TILE), 1)
    for k in range(NBLK):
        own = bo[k] // 2 == me

        @pl.when(own)
        def _():
            off = pl.multiple_of((bo[k] % 2) * blk, blk)
            cb = (bo[k] % 2) * 2
            flags = jnp.zeros((8, TILE), F32)
            for tt in range(16):
                pr = (1 - keep_ref[cb + tt % 2, tt // 2]).astype(F32)
                flags = jnp.where(jnp.logical_and(row == k, lane == tt), pr, flags)
            gc_ref[GROWS] = gc_ref[GROWS] + flags
            for half in range(2):
                d = d_ref[0:1, pl.ds(pl.multiple_of(off + half * TILE, TILE), TILE)]
                gc_ref[GROWS + 1, pl.ds(2 * k + half, 1), :] = d

        for p, (j, kk) in enumerate(PAIRS):
            if kk != k:
                continue

            @pl.when(own)
            def _():
                for half in range(2):
                    cols = pl.ds(pl.multiple_of((bo[k] % 2) * blk + half * TILE, TILE), TILE)
                    d = d_ref[0:1, cols]
                    for rh in range(2):
                        gc_ref[p * 4 + half * 2 + rh] = f_ref[j, pl.ds(rh * 8, 8), cols] * d

    moves[4].wait()
    for i, (own, lb, out) in enumerate(jobs):

        @pl.when(own)
        def _():
            if i == 2:
                out[...] = jnp.zeros((ROWS, TILE), F32)
            base = pl.multiple_of(lb * blk, blk)
            cnt = jnp.int32(0)
            for tt in range(16):
                r, cc = tt // 2, tt % 2
                pr = 1 - keep_ref[lb * 2 + cc, r]

                @pl.when(pr == 1)
                def _():
                    rows = pl.ds(pl.multiple_of(cnt * TILE, TILE), TILE)
                    out[rows, :] = w[pl.ds(r * TILE, TILE), pl.ds(base + cc * TILE, TILE)]

                cnt = jnp.minimum(cnt + pr, MAXP - 1 if tt == 15 else MAXP)


def exchange(m, ce, gc_hbm, f_hbm, t_out, f_out, g_out, fl_out,
             om, mq, gc, rb1, sb2, rb2, grb, gf,
             loc, fl_sem, f_s, f_r, fc_s, fc_r, g_s, g_r, gc_s, gc_r, grs_s, grs_r, gag_s, gag_r,
             sc_s, sc_r, r1_s, r1_r, r2_s, r2_r, a1_s, a1_r, a2_s, a2_r, ex_s, ex_r, z_s, zp_r, zm_r, zl_r):
    o = lax.axis_index("out")
    me = lax.axis_index("in")
    y, c = o // 2, o % 2
    z, x = me // NX, me % NX
    last = NIN - 1
    is_root = jnp.logical_or(me == 0, me == last)

    gcopy = pltpu.make_async_copy(gc_hbm, gc, loc.at[0])
    gcopy.start()
    mcopy = pltpu.make_async_copy(m.at[:, :, pl.ds(pl.multiple_of(x * CH, 8), CH)], mq, loc.at[1])
    mcopy.start()
    fown = pltpu.make_async_copy(f_hbm, f_out.at[o], loc.at[2])
    fown.start()

    def ydev(dy):
        return (lax.rem(y + dy, NY) * 2 + c, me)

    def zdev(dz):
        return (o, lax.rem(z + dz, NZ) * NX + x)

    def xdev(dx):
        return (o, z * NX + lax.rem(x + dx, NX))

    other = (y * 2 + 1 - c, me)

    def send(src, dst, ssem, rsem, dev):
        pltpu.make_async_remote_copy(
            src_ref=src, dst_ref=dst, send_sem=ssem, recv_sem=rsem, device_id=dev, device_id_type=MESH
        ).start()

    barrier = pltpu.get_barrier_semaphore()

    def greet(r, _):
        pl.semaphore_signal(barrier, inc=1, device_id=(o, lax.rem(me + r, NIN)), device_id_type=MESH)
        return 0

    lax.fori_loop(1, NIN, greet, 0)
    for dy in range(1, NY):
        pl.semaphore_signal(barrier, inc=1, device_id=ydev(dy), device_id_type=MESH)
    pl.semaphore_signal(barrier, inc=1, device_id=other, device_id_type=MESH)
    pl.semaphore_wait(barrier, NIN - 1 + NY - 1 + 1)

    for e in range(2):
        root = e * last

        @pl.when(me == root)
        def _():
            def scatter(r, _):
                peer = lax.rem(me + r, NIN)
                rows = pl.ds(pl.multiple_of(peer * CH, 8), CH)
                send(ce.at[rows], t_out.at[e, rows], sc_s, sc_r.at[e], (o, peer))
                return 0

            lax.fori_loop(1, NIN, scatter, 0)

    gcopy.wait()

    def spread_g(r, _):
        peer = lax.rem(me + r, NIN)
        send(gc.at[peer], grb.at[r], grs_s, grs_r, (o, peer))
        return 0

    lax.fori_loop(1, NIN, spread_g, 0)

    for dz in FAR + (0,):
        for dx in range(1, NX):
            part = pl.ds(pl.multiple_of(lax.rem(x + dx, NX) * CH, 8), CH)
            send(m.at[:, lax.rem(z + dz, NZ), part], rb1.at[dz, dx - 1], r1_s, r1_r.at[dz], xdev(dx))

    def yslot(dst, dy):
        return dst.at[lax.rem(y + NY - dy, NY) * 2 + c]

    def y_start(src, dst, ssem, rsem, csem, crsem):
        for dy in (1, NY - 1, 2, NY - 2):
            send(src, dst.at[o], ssem, rsem.at[dy - 1], ydev(dy))
        send(src, dst.at[o], csem, crsem, other)

    def y_onward(dst, ssem, rsem, csem, crsem):
        for dy, hops in ((2, ((1, 3), (2, 4))), (NY - 2, ((NY - 1, NY - 3),))):
            src = yslot(dst, dy)
            wait_for(src, rsem.at[dy - 1])
            for hop, total in hops:
                send(src, src, ssem, rsem.at[total - 1], ydev(hop))
            send(src, src, csem, crsem, other)

    def y_finish(dst, rsem, csem, crsem):
        for dy in (1, NY - 1, 3, NY - 3, 4):
            src = yslot(dst, dy)
            wait_for(src, rsem.at[dy - 1])
            send(src, src, csem, crsem, other)

    y_start(f_hbm, f_out, f_s, f_r, fc_s, fc_r)

    def chunk(dz, dx):
        h = lax.rem(z + NZ - dz, NZ) * NX + lax.rem(x + NX - dx, NX)
        return pl.ds(pl.multiple_of(h * CH, 8), CH)

    mine = chunk(0, 0)

    pair = pl.ds(2, 2)

    def from_z(dz, src):
        dst = t_out.at[pair, chunk(dz, 0)]
        for dx in range(1, NX):
            send(src, dst, a2_s, a2_r, xdev(dx))

    def zrow(dz, e=pl.ds(0, 2)):
        return t_out.at[e, pl.ds(pl.multiple_of(lax.rem(z + NZ - dz, NZ) * NX * CH, 8), NX * CH)]

    def round_z(n):
        if n:
            wait_for(zrow(n), zp_r.at[n - 1])
            wait_for(zrow(NZ - n), zm_r.at[n - 1])
        if n < NZ // 2 - 1:
            send(zrow(n), zrow(n), z_s, zp_r.at[n], zdev(1))
            send(zrow(NZ - n), zrow(NZ - n), z_s, zm_r.at[n], zdev(NZ - 1))
        else:
            send(zrow(n, 0), zrow(n, 0), z_s, zl_r.at[0], zdev(1))
            send(zrow(NZ - n, 1), zrow(NZ - n, 1), z_s, zl_r.at[1], zdev(NZ - 1))

    wait_for(grb.at[pl.ds(1, NIN - 1)], grs_r)
    grb[0] = gc[me]
    gf[me] = jnp.sum(grb[...], axis=0)

    def back_g(r, _):
        send(gf.at[me], gf.at[me], gag_s, gag_r, (o, lax.rem(me + r, NIN)))
        return 0

    lax.fori_loop(1, NIN, back_g, 0)

    for e in range(2):
        root = e * last

        @pl.when(me == root)
        def _():
            own = pltpu.make_async_copy(ce.at[mine], t_out.at[e, mine], loc.at[4])
            own.start()
            own.wait()

        @pl.when(me != root)
        def _():
            wait_for(t_out.at[e, mine], sc_r.at[e])

    for dx in range(1, NX):
        send(t_out.at[pl.ds(0, 2), mine], t_out.at[pl.ds(0, 2), mine], ex_s, ex_r, xdev(dx))

    mcopy.wait()
    y_onward(f_out, f_s, f_r, fc_s, fc_r)

    for dz in FAR + (0,):
        wait_for(rb1.at[dz], r1_r.at[dz])
        acc = mq[:, lax.rem(z + dz, NZ)]
        for q in range(NX - 1):
            acc = acc + rb1[dz, q]
        sb2[dz] = acc
        if dz:
            send(sb2.at[dz], rb2.at[dz - 1], r2_s, r2_r, zdev(dz))

    wait_for(t_out.at[pl.ds(0, 2), pl.ds(0, (NX - 1) * CH)], ex_r)
    round_z(0)

    wait_for(gf.at[pl.ds(1, NIN - 1)], gag_r)
    gown = pltpu.make_async_copy(gf.at[pl.ds(0, GROWS)], g_out.at[o], loc.at[3])
    gown.start()
    flc = pltpu.make_async_copy(gf.at[pl.ds(GROWS, 2)], fl_out, fl_sem)
    flc.start()
    y_start(gf.at[pl.ds(0, GROWS)], g_out, g_s, g_r, gc_s, gc_r)

    wait_for(rb2, r2_r)
    om[...] = sb2[0] + jnp.sum(rb2[...], axis=0)
    for dz in NEAR:
        send(om, t_out.at[pair, mine], a1_s, a1_r.at[dz - 1], zdev(dz))
    from_z(0, om)
    omc = pltpu.make_async_copy(om, t_out.at[pair, mine], loc.at[5])
    omc.start()
    round_z(1)
    y_finish(f_out, f_r, fc_s, fc_r)
    for n, dz in enumerate(NEAR):
        wait_for(t_out.at[pair, chunk(dz, 0)], a1_r.at[dz - 1])
        from_z(dz, t_out.at[pair, chunk(dz, 0)])
        if n == 2:
            round_z(2)
    y_onward(g_out, g_s, g_r, gc_s, gc_r)
    round_z(3)
    y_finish(g_out, g_r, gc_s, gc_r)

    wait_for(zrow(4, 0), zl_r.at[0])
    wait_for(zrow(4, 1), zl_r.at[1])
    wait_for(t_out.at[pair, pl.ds(0, 3 * NZ * CH)], a2_r)
    wait_for(f_out.at[pl.ds(0, NY)], fc_r)
    wait_for(g_out.at[pl.ds(0, NY)], gc_r)
    omc.wait()
    fown.wait()
    gown.wait()
    flc.wait()
    wait_for(f_out.at[pl.ds(0, NY - 1)], f_s)
    wait_for(f_out.at[pl.ds(0, NY)], fc_s)
    wait_for(g_out.at[pl.ds(0, NY - 1)], g_s)
    wait_for(g_out.at[pl.ds(0, NY)], gc_s)
    wait_for(grb.at[pl.ds(1, NIN - 1)], grs_s)
    wait_for(grb.at[pl.ds(1, NIN - 1)], gag_s)
    wait_for(rb1.at[:], r1_s)
    wait_for(rb2, r2_s)
    wait_for(t_out.at[pair, pl.ds(0, (NZ - 1) * CH)], a1_s)
    wait_for(t_out.at[pair, pl.ds(0, 3 * NZ * CH)], a2_s)
    wait_for(t_out.at[pl.ds(0, 2), pl.ds(0, (NX - 1) * CH)], ex_s)
    wait_for(t_out.at[pl.ds(0, 2), pl.ds(0, (NZ - 1) * NX * CH)], z_s)

    @pl.when(is_root)
    def _():
        wait_for(ce.at[pl.ds(CH, (NIN - 1) * CH)], sc_s)


def split(v):
    hi = v.astype(jnp.bfloat16)
    return hi, (v - hi.astype(F32)).astype(jnp.bfloat16)


def dot(a, b):
    return jnp.dot(a, b, preferred_element_type=F32)


def compensate(rt, bo_ref, keep_ref, fl_ref, dv_ref, t_ref, f_ref, g_ref, w_ref, o_hbm, f3, g3, e3, ob, start, osem):
    me = lax.axis_index("in")
    blk = 2 * TILE
    bo = [bo_ref[k] for k in range(NBLK)]

    for k in range(NBLK):
        for lb in range(2):
            b = me * 2 + lb
            done = bo[0] == b
            for j in range(1, k + 1):
                done = jnp.logical_or(done, bo[j] == b)
            v = f_ref[:, k, :, pl.ds(lb * blk, blk)].reshape(blk, blk)
            hi, lo = split(jnp.where(done, 0.0, v))
            for n, part in enumerate((hi, hi, lo)):
                f3[pl.ds((3 * k + n) * blk, blk), pl.ds(lb * blk, blk)] = part
    for p, (j, k) in enumerate(PAIRS):
        for half in range(2):
            v = g_ref[:, pl.ds(p * 4 + half * 2, 2)].reshape(blk, TILE)
            hi, lo = split(v)
            for n, part in enumerate((hi, hi, lo)):
                g3[k - 1, pl.ds((3 * j + n) * blk, blk), pl.ds(half * TILE, TILE)] = part

    srcs = []
    seen = jnp.int32(0)
    for k in range(NBLK):
        is_first, is_last = bo[k] == 0, bo[k] == 2 * NIN - 1
        srcs.append(jnp.where(is_first, 0, jnp.where(is_last, 1, 2 + seen)))
        seen = seen + jnp.where(jnp.logical_or(is_first, is_last), 0, 1)
        base = jnp.int32(0)
        for tt in range(16):
            on = fl_ref[0, k, tt] > 0.5
            start[k, tt] = jnp.where(on, base, -1)
            base = base + jnp.where(on, TILE, 0)

    nb = w_ref.shape[0] // (rt * TILE)
    br = rt * TILE
    for k in range(NBLK):
        for i in range(nb):
            acc = dot(e3[pl.ds(i * br, br), : 3 * k * blk], g3[k - 1, : 3 * k * blk]) if k else None
            for r in range(rt):
                for cc in range(2):
                    base = start[k, (i * rt + r) * 2 + cc]
                    rows = pl.ds(pl.multiple_of(jnp.maximum(base, 0), TILE), TILE)
                    v = t_ref[srcs[k], rows, :] * dv_ref[1, 2 * k + cc : 2 * k + cc + 1, :]
                    if acc is not None:
                        v = v - acc[r * TILE : (r + 1) * TILE, cc * TILE : (cc + 1) * TILE]
                    hi, lo = split(jnp.where(base >= 0, v, 0.0))
                    for n, part in enumerate((hi, lo, hi)):
                        e3[pl.ds(i * br + r * TILE, TILE), pl.ds((3 * k + n) * blk + cc * TILE, TILE)] = part

    copies = []
    for i in range(nb):
        upd = dot(e3[pl.ds(i * br, br), :], f3[...])
        for cc in range(4):
            b = me * 2 + cc // 2
            done = bo[0] == b
            for j in range(1, NBLK):
                done = jnp.logical_or(done, bo[j] == b)
            for r in range(rt):
                kept = jnp.where(done, keep_ref[cc, i * rt + r], 1).astype(F32)
                at = (pl.ds(i * br + r * TILE, TILE), pl.ds(cc * TILE, TILE))
                ob[at] = (w_ref[at] - upd[r * TILE : (r + 1) * TILE, cc * TILE : (cc + 1) * TILE]) * kept
        rows = pl.ds(i * br, br)
        copies.append(pltpu.make_async_copy(ob.at[rows], o_hbm.at[rows], osem.at[i]))
        copies[-1].start()
    for copy in copies:
        copy.wait()


def body(weight, keep_tiles, factor_rows, diag_inverse, block_order):
    rows, cols = weight.shape
    fshape = factor_rows.shape
    smem = pl.BlockSpec(memory_space=pltpu.SMEM)
    vmem = pl.BlockSpec(memory_space=pltpu.VMEM)
    anym = pl.BlockSpec(memory_space=pl.ANY)
    hbm = pl.BlockSpec(memory_space=pltpu.HBM)
    dma = pltpu.SemaphoreType.DMA
    one = dma(())
    mids, ends, shares = pl.pallas_call(
        stage,
        out_shape=(
            jax.ShapeDtypeStruct((2, ROWS, TILE), F32),
            jax.ShapeDtypeStruct((ROWS, TILE), F32),
            jax.ShapeDtypeStruct((NIN, 8, TILE), F32),
        ),
        in_specs=[hbm] * 5,
        out_specs=(vmem, vmem, vmem),
        scratch_shapes=[
            pltpu.SMEM(block_order.shape, jnp.int32),
            pltpu.SMEM(keep_tiles.T.shape, jnp.int32),
            pltpu.VMEM((rows, cols), F32),
            pltpu.VMEM(fshape, F32),
            pltpu.VMEM((1, cols), F32),
            dma((5,)),
        ],
        compiler_params=pltpu.CompilerParams(vmem_limit_bytes=12 << 20),
    )(block_order, keep_tiles.T, weight, factor_rows, diag_inverse.reshape(1, cols))
    tiles, facs, pans, flags = pl.pallas_call(
        exchange,
        out_shape=(
            jax.ShapeDtypeStruct((NBLK, ROWS, TILE), F32),
            jax.ShapeDtypeStruct((NOUT,) + fshape, F32),
            jax.ShapeDtypeStruct((NOUT, GROWS, 8, TILE), F32),
            jax.ShapeDtypeStruct((2, 8, TILE), F32),
        ),
        in_specs=[anym, anym, anym, anym],
        out_specs=(anym, anym, anym, anym),
        scratch_shapes=[
            pltpu.VMEM((2, CH, TILE), F32),
            pltpu.VMEM((2, NZ, CH, TILE), F32),
            pltpu.VMEM((NIN, 8, TILE), F32),
            pltpu.VMEM((NZ, NX - 1, 2, CH, TILE), F32),
            pltpu.VMEM((NZ, 2, CH, TILE), F32),
            pltpu.VMEM((NZ - 1, 2, CH, TILE), F32),
            pltpu.VMEM((NIN, 8, TILE), F32),
            pltpu.VMEM((NIN, 8, TILE), F32),
            dma((6,)), one,
            one, dma((NY - 1,)), one, one,
            one, dma((NY - 1,)), one, one,
            one, one, one, one,
            one, dma((2,)), one, dma((NZ,)), one, one,
            one, dma((NZ - 1,)), one, one, one, one, one, dma((3,)), dma((3,)), dma((2,)),
        ],
        compiler_params=pltpu.CompilerParams(
            collective_id=0, has_side_effects=True, vmem_limit_bytes=16 << 20
        ),
    )(mids.reshape(2, NZ, NX * CH, TILE), ends, shares, factor_rows)

    rt = 4
    br = rt * TILE
    depth = NBLK * 2 * TILE
    bf16 = jnp.bfloat16
    return pl.pallas_call(
        lambda *refs: compensate(rt, *refs),
        out_shape=jax.ShapeDtypeStruct((rows, cols), F32),
        in_specs=[smem, smem, smem, vmem, vmem, vmem, vmem, vmem],
        out_specs=anym,
        scratch_shapes=[
            pltpu.VMEM((3 * depth, cols), bf16),
            pltpu.VMEM((NBLK - 1, 3 * (NBLK - 1) * 2 * TILE, 2 * TILE), bf16),
            pltpu.VMEM((rows, 3 * depth), bf16),
            pltpu.VMEM((rows, cols), F32),
            pltpu.SMEM((NBLK, 16), jnp.int32),
            dma((rows // br,)),
        ],
        compiler_params=pltpu.CompilerParams(vmem_limit_bytes=24 << 20),
    )(block_order, keep_tiles.T, flags, flags, tiles, facs, pans, weight)


def solution(mesh):
    return jax.shard_map(
        body,
        mesh=mesh,
        in_specs=(P("out", "in"), P("out", "in"), P(None, "out", "in"), P("in"), P()),
        out_specs=P("out", "in"),
        check_vma=False,
    )
```

```python
import jax
import jax.numpy as jnp
from jax import lax
from jax.experimental import pallas as pl
from jax.experimental.pallas import tpu as pltpu
from jax.sharding import PartitionSpec as P

MESH = pl.DeviceIdType.MESH
TILE = 128
NBLK = 4
MAXP = 10
NZ, NX, NY = 8, 4, 8
NIN, NOUT = NZ * NX, NY * 2
ROWS = MAXP * TILE
CH = ROWS // NIN
PAIRS = [(j, k) for k in range(NBLK) for j in range(k)]
GROWS = len(PAIRS) * 4
F32 = jnp.float32
NEAR = (1, 7, 2, 6, 3, 5, 4)
FAR = (4, 3, 5, 2, 6, 1, 7)


def wait_for(ref, sem):
    pltpu.make_async_copy(ref, ref, sem).wait()


def stage(bo_hbm, keep_hbm, w_hbm, f_hbm, d_hbm, m_out, ce_out, gc_ref, bo_ref, keep_ref, w, f_ref, d_ref, sem):
    moves = [
        pltpu.make_async_copy(src, dst, sem.at[i])
        for i, (src, dst) in enumerate(
            ((bo_hbm, bo_ref), (keep_hbm, keep_ref), (d_hbm, d_ref), (f_hbm, f_ref), (w_hbm, w))
        )
    ]
    for move in moves:
        move.start()
    me = lax.axis_index("in")
    last = NIN - 1
    blk = 2 * TILE
    m_out[...] = jnp.zeros_like(m_out)
    gc_ref[...] = jnp.zeros_like(gc_ref)
    for move in moves[:4]:
        move.wait()
    first_b, last_b = 0, 2 * NIN - 1
    bo = [bo_ref[k] for k in range(NBLK)]
    mid = [jnp.int32(0), jnp.int32(0)]
    seen = jnp.int32(0)
    for k in range(NBLK):
        is_mid = jnp.logical_and(bo[k] != first_b, bo[k] != last_b)
        for q in range(2):
            mid[q] = jnp.where(jnp.logical_and(is_mid, seen == q), bo[k], mid[q])
        seen = seen + is_mid.astype(jnp.int32)
    is_root = jnp.logical_or(me == 0, me == last)
    jobs = [
        (mid[0] // 2 == me, mid[0] % 2, m_out.at[0]),
        (mid[1] // 2 == me, mid[1] % 2, m_out.at[1]),
        (is_root, jnp.where(me == last, 1, 0), ce_out),
    ]

    row = lax.broadcasted_iota(jnp.int32, (8, TILE), 0)
    lane = lax.broadcasted_iota(jnp.int32, (8, TILE), 1)
    for k in range(NBLK):
        own = bo[k] // 2 == me

        @pl.when(own)
        def _():
            off = pl.multiple_of((bo[k] % 2) * blk, blk)
            cb = (bo[k] % 2) * 2
            flags = jnp.zeros((8, TILE), F32)
            for tt in range(16):
                pr = (1 - keep_ref[cb + tt % 2, tt // 2]).astype(F32)
                flags = jnp.where(jnp.logical_and(row == k, lane == tt), pr, flags)
            gc_ref[GROWS] = gc_ref[GROWS] + flags
            for half in range(2):
                d = d_ref[0:1, pl.ds(pl.multiple_of(off + half * TILE, TILE), TILE)]
                gc_ref[GROWS + 1, pl.ds(2 * k + half, 1), :] = d

        for p, (j, kk) in enumerate(PAIRS):
            if kk != k:
                continue

            @pl.when(own)
            def _():
                for half in range(2):
                    cols = pl.ds(pl.multiple_of((bo[k] % 2) * blk + half * TILE, TILE), TILE)
                    d = d_ref[0:1, cols]
                    for rh in range(2):
                        gc_ref[p * 4 + half * 2 + rh] = f_ref[j, pl.ds(rh * 8, 8), cols] * d

    moves[4].wait()
    for i, (own, lb, out) in enumerate(jobs):

        @pl.when(own)
        def _():
            if i == 2:
                out[...] = jnp.zeros((ROWS, TILE), F32)
            base = pl.multiple_of(lb * blk, blk)
            cnt = jnp.int32(0)
            for tt in range(16):
                r, cc = tt // 2, tt % 2
                pr = 1 - keep_ref[lb * 2 + cc, r]

                @pl.when(pr == 1)
                def _():
                    rows = pl.ds(pl.multiple_of(cnt * TILE, TILE), TILE)
                    out[rows, :] = w[pl.ds(r * TILE, TILE), pl.ds(base + cc * TILE, TILE)]

                cnt = jnp.minimum(cnt + pr, MAXP - 1 if tt == 15 else MAXP)


def exchange(m, ce, gc_hbm, f_hbm, t_out, f_out, g_out, fl_out,
             om, mq, gc, rb1, sb2, rb2, grb, gf,
             loc, fl_sem, f_s, f_r, fc_s, fc_r, g_s, g_r, gc_s, gc_r, grs_s, grs_r, gag_s, gag_r,
             sc_s, sc_r, r1_s, r1_r, r2_s, r2_r, a1_s, a1_r, a2_s, a2_r, ex_s, ex_r, z_s, zp_r, zm_r, zl_r):
    o = lax.axis_index("out")
    me = lax.axis_index("in")
    y, c = o // 2, o % 2
    z, x = me // NX, me % NX
    last = NIN - 1
    is_root = jnp.logical_or(me == 0, me == last)

    gcopy = pltpu.make_async_copy(gc_hbm, gc, loc.at[0])
    gcopy.start()
    mcopy = pltpu.make_async_copy(m.at[:, :, pl.ds(pl.multiple_of(x * CH, 8), CH)], mq, loc.at[1])
    mcopy.start()
    fown = pltpu.make_async_copy(f_hbm, f_out.at[o], loc.at[2])
    fown.start()

    def ydev(dy):
        return (lax.rem(y + dy, NY) * 2 + c, me)

    def zdev(dz):
        return (o, lax.rem(z + dz, NZ) * NX + x)

    def xdev(dx):
        return (o, z * NX + lax.rem(x + dx, NX))

    other = (y * 2 + 1 - c, me)

    def send(src, dst, ssem, rsem, dev):
        pltpu.make_async_remote_copy(
            src_ref=src, dst_ref=dst, send_sem=ssem, recv_sem=rsem, device_id=dev, device_id_type=MESH
        ).start()

    barrier = pltpu.get_barrier_semaphore()

    def greet(r, _):
        pl.semaphore_signal(barrier, inc=1, device_id=(o, lax.rem(me + r, NIN)), device_id_type=MESH)
        return 0

    lax.fori_loop(1, NIN, greet, 0)
    for dy in range(1, NY):
        pl.semaphore_signal(barrier, inc=1, device_id=ydev(dy), device_id_type=MESH)
    pl.semaphore_signal(barrier, inc=1, device_id=other, device_id_type=MESH)
    pl.semaphore_wait(barrier, NIN - 1 + NY - 1 + 1)

    for e in range(2):
        root = e * last

        @pl.when(me == root)
        def _():
            def scatter(r, _):
                peer = lax.rem(me + r, NIN)
                rows = pl.ds(pl.multiple_of(peer * CH, 8), CH)
                send(ce.at[rows], t_out.at[e, rows], sc_s, sc_r.at[e], (o, peer))
                return 0

            lax.fori_loop(1, NIN, scatter, 0)

    gcopy.wait()

    def spread_g(r, _):
        peer = lax.rem(me + r, NIN)
        send(gc.at[peer], grb.at[r], grs_s, grs_r, (o, peer))
        return 0

    lax.fori_loop(1, NIN, spread_g, 0)

    for dz in NEAR + (0,):
        for dx in range(1, NX):
            part = pl.ds(pl.multiple_of(lax.rem(x + dx, NX) * CH, 8), CH)
            send(m.at[:, lax.rem(z + dz, NZ), part], rb1.at[dz, dx - 1], r1_s, r1_r.at[dz], xdev(dx))

    def yslot(dst, dy):
        return dst.at[lax.rem(y + NY - dy, NY) * 2 + c]

    def y_start(src, dst, ssem, rsem, csem, crsem):
        for dy in (1, NY - 1, 2, NY - 2):
            send(src, dst.at[o], ssem, rsem.at[dy - 1], ydev(dy))
        send(src, dst.at[o], csem, crsem, other)

    def y_onward(dst, ssem, rsem, csem, crsem):
        for dy, hops in ((2, ((1, 3), (2, 4))), (NY - 2, ((NY - 1, NY - 3),))):
            src = yslot(dst, dy)
            wait_for(src, rsem.at[dy - 1])
            for hop, total in hops:
                send(src, src, ssem, rsem.at[total - 1], ydev(hop))
            send(src, src, csem, crsem, other)

    def y_finish(dst, rsem, csem, crsem):
        for dy in (1, NY - 1, 3, NY - 3, 4):
            src = yslot(dst, dy)
            wait_for(src, rsem.at[dy - 1])
            send(src, src, csem, crsem, other)

    y_start(f_hbm, f_out, f_s, f_r, fc_s, fc_r)

    def chunk(dz, dx):
        h = lax.rem(z + NZ - dz, NZ) * NX + lax.rem(x + NX - dx, NX)
        return pl.ds(pl.multiple_of(h * CH, 8), CH)

    mine = chunk(0, 0)

    pair = pl.ds(2, 2)

    def from_z(dz, src):
        dst = t_out.at[pair, chunk(dz, 0)]
        for dx in range(1, NX):
            send(src, dst, a2_s, a2_r, xdev(dx))

    def zrow(dz, e=pl.ds(0, 2)):
        return t_out.at[e, pl.ds(pl.multiple_of(lax.rem(z + NZ - dz, NZ) * NX * CH, 8), NX * CH)]

    def round_z(n):
        if n:
            wait_for(zrow(n), zp_r.at[n - 1])
            wait_for(zrow(NZ - n), zm_r.at[n - 1])
        if n < NZ // 2 - 1:
            send(zrow(n), zrow(n), z_s, zp_r.at[n], zdev(1))
            send(zrow(NZ - n), zrow(NZ - n), z_s, zm_r.at[n], zdev(NZ - 1))
        else:
            send(zrow(n, 0), zrow(n, 0), z_s, zl_r.at[0], zdev(1))
            send(zrow(NZ - n, 1), zrow(NZ - n, 1), z_s, zl_r.at[1], zdev(NZ - 1))

    wait_for(grb.at[pl.ds(1, NIN - 1)], grs_r)
    grb[0] = gc[me]
    gf[me] = jnp.sum(grb[...], axis=0)

    def back_g(r, _):
        send(gf.at[me], gf.at[me], gag_s, gag_r, (o, lax.rem(me + r, NIN)))
        return 0

    lax.fori_loop(1, NIN, back_g, 0)

    for e in range(2):
        root = e * last

        @pl.when(me == root)
        def _():
            own = pltpu.make_async_copy(ce.at[mine], t_out.at[e, mine], loc.at[4])
            own.start()
            own.wait()

        @pl.when(me != root)
        def _():
            wait_for(t_out.at[e, mine], sc_r.at[e])

    for dx in range(1, NX):
        send(t_out.at[pl.ds(0, 2), mine], t_out.at[pl.ds(0, 2), mine], ex_s, ex_r, xdev(dx))

    mcopy.wait()

    for dz in NEAR + (0,):
        wait_for(rb1.at[dz], r1_r.at[dz])
        acc = mq[:, lax.rem(z + dz, NZ)]
        for q in range(NX - 1):
            acc = acc + rb1[dz, q]
        sb2[dz] = acc
        if dz:
            send(sb2.at[dz], rb2.at[dz - 1], r2_s, r2_r, zdev(dz))

    wait_for(t_out.at[pl.ds(0, 2), pl.ds(0, (NX - 1) * CH)], ex_r)
    round_z(0)
    y_onward(f_out, f_s, f_r, fc_s, fc_r)

    wait_for(gf.at[pl.ds(1, NIN - 1)], gag_r)
    gown = pltpu.make_async_copy(gf.at[pl.ds(0, GROWS)], g_out.at[o], loc.at[3])
    gown.start()
    flc = pltpu.make_async_copy(gf.at[pl.ds(GROWS, 2)], fl_out, fl_sem)
    flc.start()
    y_start(gf.at[pl.ds(0, GROWS)], g_out, g_s, g_r, gc_s, gc_r)

    wait_for(rb2, r2_r)
    om[...] = sb2[0] + jnp.sum(rb2[...], axis=0)
    for dz in NEAR:
        send(om, t_out.at[pair, mine], a1_s, a1_r.at[dz - 1], zdev(dz))
    from_z(0, om)
    omc = pltpu.make_async_copy(om, t_out.at[pair, mine], loc.at[5])
    omc.start()
    round_z(1)
    y_finish(f_out, f_r, fc_s, fc_r)
    for n, dz in enumerate(NEAR):
        wait_for(t_out.at[pair, chunk(dz, 0)], a1_r.at[dz - 1])
        from_z(dz, t_out.at[pair, chunk(dz, 0)])
        if n == 2:
            round_z(2)
    y_onward(g_out, g_s, g_r, gc_s, gc_r)
    round_z(3)
    y_finish(g_out, g_r, gc_s, gc_r)

    wait_for(zrow(4, 0), zl_r.at[0])
    wait_for(zrow(4, 1), zl_r.at[1])
    wait_for(t_out.at[pair, pl.ds(0, 3 * NZ * CH)], a2_r)
    wait_for(f_out.at[pl.ds(0, NY)], fc_r)
    wait_for(g_out.at[pl.ds(0, NY)], gc_r)
    omc.wait()
    fown.wait()
    gown.wait()
    flc.wait()
    wait_for(f_out.at[pl.ds(0, NY - 1)], f_s)
    wait_for(f_out.at[pl.ds(0, NY)], fc_s)
    wait_for(g_out.at[pl.ds(0, NY - 1)], g_s)
    wait_for(g_out.at[pl.ds(0, NY)], gc_s)
    wait_for(grb.at[pl.ds(1, NIN - 1)], grs_s)
    wait_for(grb.at[pl.ds(1, NIN - 1)], gag_s)
    wait_for(rb1.at[:], r1_s)
    wait_for(rb2, r2_s)
    wait_for(t_out.at[pair, pl.ds(0, (NZ - 1) * CH)], a1_s)
    wait_for(t_out.at[pair, pl.ds(0, 3 * NZ * CH)], a2_s)
    wait_for(t_out.at[pl.ds(0, 2), pl.ds(0, (NX - 1) * CH)], ex_s)
    wait_for(t_out.at[pl.ds(0, 2), pl.ds(0, (NZ - 1) * NX * CH)], z_s)

    @pl.when(is_root)
    def _():
        wait_for(ce.at[pl.ds(CH, (NIN - 1) * CH)], sc_s)


def split(v):
    hi = v.astype(jnp.bfloat16)
    return hi, (v - hi.astype(F32)).astype(jnp.bfloat16)


def dot(a, b):
    return jnp.dot(a, b, preferred_element_type=F32)


def compensate(rt, bo_ref, keep_ref, fl_ref, dv_ref, t_ref, f_ref, g_ref, w_ref, o_hbm, f3, g3, e3, ob, start, osem):
    me = lax.axis_index("in")
    blk = 2 * TILE
    bo = [bo_ref[k] for k in range(NBLK)]

    for k in range(NBLK):
        for lb in range(2):
            b = me * 2 + lb
            done = bo[0] == b
            for j in range(1, k + 1):
                done = jnp.logical_or(done, bo[j] == b)
            v = f_ref[:, k, :, pl.ds(lb * blk, blk)].reshape(blk, blk)
            hi, lo = split(jnp.where(done, 0.0, v))
            for n, part in enumerate((hi, hi, lo)):
                f3[pl.ds((3 * k + n) * blk, blk), pl.ds(lb * blk, blk)] = part
    for p, (j, k) in enumerate(PAIRS):
        for half in range(2):
            v = g_ref[:, pl.ds(p * 4 + half * 2, 2)].reshape(blk, TILE)
            hi, lo = split(v)
            for n, part in enumerate((hi, hi, lo)):
                g3[k - 1, pl.ds((3 * j + n) * blk, blk), pl.ds(half * TILE, TILE)] = part

    srcs = []
    seen = jnp.int32(0)
    for k in range(NBLK):
        is_first, is_last = bo[k] == 0, bo[k] == 2 * NIN - 1
        srcs.append(jnp.where(is_first, 0, jnp.where(is_last, 1, 2 + seen)))
        seen = seen + jnp.where(jnp.logical_or(is_first, is_last), 0, 1)
        base = jnp.int32(0)
        for tt in range(16):
            on = fl_ref[0, k, tt] > 0.5
            start[k, tt] = jnp.where(on, base, -1)
            base = base + jnp.where(on, TILE, 0)

    nb = w_ref.shape[0] // (rt * TILE)
    br = rt * TILE
    for k in range(NBLK):
        for i in range(nb):
            acc = dot(e3[pl.ds(i * br, br), : 3 * k * blk], g3[k - 1, : 3 * k * blk]) if k else None
            for r in range(rt):
                for cc in range(2):
                    base = start[k, (i * rt + r) * 2 + cc]
                    rows = pl.ds(pl.multiple_of(jnp.maximum(base, 0), TILE), TILE)
                    v = t_ref[srcs[k], rows, :] * dv_ref[1, 2 * k + cc : 2 * k + cc + 1, :]
                    if acc is not None:
                        v = v - acc[r * TILE : (r + 1) * TILE, cc * TILE : (cc + 1) * TILE]
                    hi, lo = split(jnp.where(base >= 0, v, 0.0))
                    for n, part in enumerate((hi, lo, hi)):
                        e3[pl.ds(i * br + r * TILE, TILE), pl.ds((3 * k + n) * blk + cc * TILE, TILE)] = part

    copies = []
    for i in range(nb):
        upd = dot(e3[pl.ds(i * br, br), :], f3[...])
        for cc in range(4):
            b = me * 2 + cc // 2
            done = bo[0] == b
            for j in range(1, NBLK):
                done = jnp.logical_or(done, bo[j] == b)
            for r in range(rt):
                kept = jnp.where(done, keep_ref[cc, i * rt + r], 1).astype(F32)
                at = (pl.ds(i * br + r * TILE, TILE), pl.ds(cc * TILE, TILE))
                ob[at] = (w_ref[at] - upd[r * TILE : (r + 1) * TILE, cc * TILE : (cc + 1) * TILE]) * kept
        rows = pl.ds(i * br, br)
        copies.append(pltpu.make_async_copy(ob.at[rows], o_hbm.at[rows], osem.at[i]))
        copies[-1].start()
    for copy in copies:
        copy.wait()


def body(weight, keep_tiles, factor_rows, diag_inverse, block_order):
    rows, cols = weight.shape
    fshape = factor_rows.shape
    smem = pl.BlockSpec(memory_space=pltpu.SMEM)
    vmem = pl.BlockSpec(memory_space=pltpu.VMEM)
    anym = pl.BlockSpec(memory_space=pl.ANY)
    hbm = pl.BlockSpec(memory_space=pltpu.HBM)
    dma = pltpu.SemaphoreType.DMA
    one = dma(())
    mids, ends, shares = pl.pallas_call(
        stage,
        out_shape=(
            jax.ShapeDtypeStruct((2, ROWS, TILE), F32),
            jax.ShapeDtypeStruct((ROWS, TILE), F32),
            jax.ShapeDtypeStruct((NIN, 8, TILE), F32),
        ),
        in_specs=[hbm] * 5,
        out_specs=(vmem, vmem, vmem),
        scratch_shapes=[
            pltpu.SMEM(block_order.shape, jnp.int32),
            pltpu.SMEM(keep_tiles.T.shape, jnp.int32),
            pltpu.VMEM((rows, cols), F32),
            pltpu.VMEM(fshape, F32),
            pltpu.VMEM((1, cols), F32),
            dma((5,)),
        ],
        compiler_params=pltpu.CompilerParams(vmem_limit_bytes=12 << 20),
    )(block_order, keep_tiles.T, weight, factor_rows, diag_inverse.reshape(1, cols))
    tiles, facs, pans, flags = pl.pallas_call(
        exchange,
        out_shape=(
            jax.ShapeDtypeStruct((NBLK, ROWS, TILE), F32),
            jax.ShapeDtypeStruct((NOUT,) + fshape, F32),
            jax.ShapeDtypeStruct((NOUT, GROWS, 8, TILE), F32),
            jax.ShapeDtypeStruct((2, 8, TILE), F32),
        ),
        in_specs=[anym, anym, anym, anym],
        out_specs=(anym, anym, anym, anym),
        scratch_shapes=[
            pltpu.VMEM((2, CH, TILE), F32),
            pltpu.VMEM((2, NZ, CH, TILE), F32),
            pltpu.VMEM((NIN, 8, TILE), F32),
            pltpu.VMEM((NZ, NX - 1, 2, CH, TILE), F32),
            pltpu.VMEM((NZ, 2, CH, TILE), F32),
            pltpu.VMEM((NZ - 1, 2, CH, TILE), F32),
            pltpu.VMEM((NIN, 8, TILE), F32),
            pltpu.VMEM((NIN, 8, TILE), F32),
            dma((6,)), one,
            one, dma((NY - 1,)), one, one,
            one, dma((NY - 1,)), one, one,
            one, one, one, one,
            one, dma((2,)), one, dma((NZ,)), one, one,
            one, dma((NZ - 1,)), one, one, one, one, one, dma((3,)), dma((3,)), dma((2,)),
        ],
        compiler_params=pltpu.CompilerParams(
            collective_id=0, has_side_effects=True, vmem_limit_bytes=16 << 20
        ),
    )(mids.reshape(2, NZ, NX * CH, TILE), ends, shares, factor_rows)

    rt = 2
    br = rt * TILE
    depth = NBLK * 2 * TILE
    bf16 = jnp.bfloat16
    return pl.pallas_call(
        lambda *refs: compensate(rt, *refs),
        out_shape=jax.ShapeDtypeStruct((rows, cols), F32),
        in_specs=[smem, smem, smem, vmem, vmem, vmem, vmem, vmem],
        out_specs=anym,
        scratch_shapes=[
            pltpu.VMEM((3 * depth, cols), bf16),
            pltpu.VMEM((NBLK - 1, 3 * (NBLK - 1) * 2 * TILE, 2 * TILE), bf16),
            pltpu.VMEM((rows, 3 * depth), bf16),
            pltpu.VMEM((rows, cols), F32),
            pltpu.SMEM((NBLK, 16), jnp.int32),
            dma((rows // br,)),
        ],
        compiler_params=pltpu.CompilerParams(vmem_limit_bytes=24 << 20),
    )(block_order, keep_tiles.T, flags, flags, tiles, facs, pans, weight)


def solution(mesh):
    return jax.shard_map(
        body,
        mesh=mesh,
        in_specs=(P("out", "in"), P("out", "in"), P(None, "out", "in"), P("in"), P()),
        out_specs=P("out", "in"),
        check_vma=False,
    )
```
